32 devices in a mesh: grp: 2 (over y), tile: 4 (over z), date: 2 (over x), pol: 2 (over core).
Axes of the slice: x: 2, y: 2, z: 4, core: 2. Of those that a mesh axis runs over, the one named last changes fastest.
Arguments:
- stack: bfloat16 [2, 16, 3, 16384], P(None, ('date', 'pol'), None, ('grp', 'tile')), parts along dimension 3, may hold values from -40 to 40
- nbr_tile: int32 [16, 16384], P(None, ('grp', 'tile', 'date', 'pol')), parts along dimension 1, may hold values from 0 to 3, as said below
- nbr_slot: int32 [16, 16384], P(None, ('grp', 'tile', 'date', 'pol')), parts along dimension 1, may hold values from 0 to 511, as said below
- nbr_valid: int32 [16, 16384], P(None, ('grp', 'tile', 'date', 'pol')), parts along dimension 1, may hold values from 0 to 1
- fetch_rows: int32 [8, 4, 4, 128], P(('grp', 'tile'), ('date', 'pol')), parts along dimension 0, may hold values from 0 to 511
Outputs:
- linked: float32 [2, 16, 3, 16384], P(None, None, None, ('grp', 'tile', 'date', 'pol')), parts along dimension 3
The draws below stay inside these ranges and needn't reach their ends.
There are 2 independent parts, one for each index of `grp`. The reference program is written for one: setup_inputs(seed, part) draws one part's arguments, and reference() takes and returns one part's arrays. A program takes and returns all parts, laid end to end along the dimension named above; each array names one. Nothing has to cross between parts.
Inputs may be any that keep to these rules, and one draw needn't show every extreme that they name: `nbr_tile`: entry 0 of every pixel names the pixel's own tile. `nbr_slot`: where nbr_tile is the pixel's own tile, a row of the pixel's own block, entry 0 being the pixel itself; elsewhere a slot of the fetch list of the pixel's block toward that tile.
All inputs are finite; a program needn't handle non-finite values.
Results may differ from the reference program's by a relative error of at most 0.0003.
Values may be sent and summed in bfloat16 or wider, within the bound.
A program may use at most 64 MiB of HBM per device.

```python
import math
import jax
import jax.numpy as jnp
from jax import lax

DATES = 16
POLS = 3
CHANNELS = 48
PIX_DEV = 512
NEIGH = 16
FETCH_CAP = 128
POWER_ITERS = 8
STRIPS = 4
PIXELS = 8192
N_TILE = 4


def neighbour_lists(key):
    live_key, side_key, peer_key, slot_key, valid_key = jax.random.split(key, 5)
    blocks = N_TILE * STRIPS
    live = jax.random.randint(live_key, (blocks, N_TILE), max(1, FETCH_CAP // 4), FETCH_CAP + 1)
    block_home = jnp.arange(blocks, dtype=jnp.int32) // STRIPS
    next_tile = (block_home + 1) % N_TILE
    live = jnp.where(jnp.arange(N_TILE, dtype=jnp.int32)[None, :] == next_tile[:, None], FETCH_CAP, live)
    column = jnp.arange(PIXELS, dtype=jnp.int32)
    block = column // PIX_DEV
    home = block // STRIPS
    side = jax.random.randint(side_key, (NEIGH, PIXELS), 0, 2)
    step = jax.random.randint(peer_key, (NEIGH, PIXELS), 1, N_TILE)
    peer = jnp.where(side == 1, (home[None, :] + step) % N_TILE, home[None, :])
    peer = peer.at[0].set(home)
    count = jnp.where(peer == home[None, :], PIX_DEV, live[block[None, :], peer])
    raw = jax.random.randint(slot_key, (NEIGH, PIXELS), 0, 2 ** 30)
    slot = raw % count
    slot = slot.at[0].set(column % PIX_DEV)
    valid = (jax.random.randint(valid_key, (NEIGH, PIXELS), 0, 8) > 0).astype(jnp.int32)
    valid = valid.at[0].set(1)
    return (peer.astype(jnp.int32), slot.astype(jnp.int32), valid)


def draw_nbr_tile(key, part):
    return neighbour_lists(key)[0]


def draw_nbr_slot(key, part):
    return neighbour_lists(key)[1]


def draw_nbr_valid(key, part):
    return neighbour_lists(key)[2]


def draw_fetch_rows(key, part):
    key = jax.random.fold_in(key, 7)
    return jax.random.randint(key, (N_TILE, STRIPS, N_TILE, FETCH_CAP), 0, PIX_DEV).astype(jnp.int32)


def draw_stack(key, part):
    key = jax.random.fold_in(key, 5)
    noise_key, scale_key = jax.random.split(key, 2)
    shape = (2, DATES, POLS, PIXELS)
    scale = jnp.exp(jax.random.uniform(scale_key, (1, DATES, POLS, 1), minval=0.0, maxval=math.log(10.0)))
    values = jnp.clip(jax.random.normal(noise_key, shape), -4.0, 4.0) * scale
    return jnp.clip(values, -40.0, 40.0).astype(jnp.bfloat16)


def setup_inputs(seed: int = 0, part: int = 0) -> dict:
    keys = jax.random.split(jax.random.key(seed), 6)
    own_keys = jax.random.split(jax.random.fold_in(keys[5], part), 6)
    return {
        "stack": draw_stack(jax.random.fold_in(jax.random.fold_in(keys[5], part), 71), part),
        "nbr_tile": draw_nbr_tile(jax.random.fold_in(jax.random.fold_in(keys[5], part), 71), part),
        "nbr_slot": draw_nbr_slot(jax.random.fold_in(jax.random.fold_in(keys[5], part), 71), part),
        "nbr_valid": draw_nbr_valid(jax.random.fold_in(jax.random.fold_in(keys[5], part), 71), part),
        "fetch_rows": draw_fetch_rows(jax.random.fold_in(jax.random.fold_in(keys[5], part), 71), part),
    }


eps = 1e-06
floor_value = 0.3

def phase_link_rows(gram, start_rows):
    highest = lax.Precision.HIGHEST
    real_part = gram[:, :CHANNELS, :CHANNELS] + gram[:, CHANNELS:, CHANNELS:]
    cross = gram[:, :CHANNELS, CHANNELS:]
    imag_part = jnp.transpose(cross, (0, 2, 1)) - cross
    vec_real = start_rows[:, :CHANNELS]
    vec_imag = start_rows[:, CHANNELS:]
    for turn in range(POWER_ITERS):
        new_real = jnp.einsum('bij,bj->bi', real_part, vec_real, precision=highest) - jnp.einsum('bij,bj->bi', imag_part, vec_imag, precision=highest)
        new_imag = jnp.einsum('bij,bj->bi', imag_part, vec_real, precision=highest) + jnp.einsum('bij,bj->bi', real_part, vec_imag, precision=highest)
        factor = lax.rsqrt(lax.optimization_barrier(jnp.sum(new_real * new_real + new_imag * new_imag, axis=1)) / CHANNELS + eps)
        vec_real = new_real * factor[:, None]
        vec_imag = new_imag * factor[:, None]
    first_real = vec_real[:, :1]
    first_imag = vec_imag[:, :1]
    denom = jnp.maximum(jnp.sqrt(first_real * first_real + first_imag * first_imag), floor_value)
    out_real = (vec_real * first_real + vec_imag * first_imag) / denom
    out_imag = (vec_imag * first_real - vec_real * first_imag) / denom
    return jnp.stack([out_real, out_imag], axis=1)

def reference(stack, nbr_tile, nbr_slot, nbr_valid, fetch_rows):
    table = stack.reshape(2 * CHANNELS, PIXELS).astype(jnp.float32).T
    column = jnp.arange(PIXELS, dtype=jnp.int32)
    block = column // PIX_DEV
    home = block // STRIPS
    strip = block % STRIPS
    flat_requests = fetch_rows.reshape(-1).astype(jnp.int32)
    lookup = ((home[None, :] * STRIPS + strip[None, :]) * N_TILE + nbr_tile) * FETCH_CAP + jnp.minimum(nbr_slot, FETCH_CAP - 1)
    remote_rows = flat_requests[lookup.astype(jnp.int32)]
    row_in_block = jnp.where(nbr_tile == home[None, :], nbr_slot, remote_rows)
    source = ((nbr_tile * STRIPS + strip[None, :]) * PIX_DEV + row_in_block).astype(jnp.int32)
    mask = nbr_valid.astype(jnp.float32)
    span = PIX_DEV * STRIPS

    def one_tile(number):
        begin = (number * span).astype(jnp.int32)
        chosen = lax.dynamic_slice_in_dim(source, begin, span, 1).T
        keep = lax.dynamic_slice_in_dim(mask, begin, span, 1).T
        near = table[chosen] * keep[:, :, None]
        gram = jnp.einsum('bkf,bkg->bfg', near, near, precision=lax.Precision.HIGHEST)
        start_rows = lax.dynamic_slice_in_dim(table, begin, span, 0)
        return phase_link_rows(gram, start_rows)
    linked = lax.map(one_tile, jnp.arange(N_TILE, dtype=jnp.int32))
    linked = jnp.transpose(linked.reshape(PIXELS, 2, CHANNELS), (1, 2, 0))
    return linked.reshape(2, DATES, POLS, PIXELS)
```

```python
import functools

import jax
import jax.numpy as jnp
from jax import lax
from jax.experimental import pallas as pl
from jax.experimental.pallas import tpu as pltpu
from jax.sharding import PartitionSpec as P

POWER_ITERS = 8
LANES = 128
PIECE = 256
MESH = pl.DeviceIdType.MESH

eps = 1e-06
floor_value = 0.3


def one_hot(index, rows):
    row = lax.broadcasted_iota(jnp.int32, (rows, index.shape[1]), 0)
    return jnp.where(row == index, 1.0, 0.0).astype(jnp.bfloat16)


def gather_kernel(dates, pols, tiles, stack_ref, wanted_ref, table_ref, fetched_ref,
                  outbox, inbox, asked, picked,
                  out_sem, in_sem, ask_sem, asked_sem, pick_sem, fetch_sem):
    strips = dates * pols
    parts, sets, local, _ = stack_ref.shape
    rows = parts * sets * local
    width = table_ref.shape[1]
    capacity = wanted_ref.shape[-1]
    date, pol, tile = lax.axis_index("date"), lax.axis_index("pol"), lax.axis_index("tile")
    me = date * pols + pol

    barrier = pltpu.get_barrier_semaphore()
    for step in range(1, strips):
        peer = lax.rem(me + step, strips)
        pl.semaphore_signal(barrier, inc=1, device_id={"date": peer // pols, "pol": lax.rem(peer, pols)},
                            device_id_type=MESH)
    for step in range(1, tiles):
        pl.semaphore_signal(barrier, inc=1, device_id={"tile": lax.rem(tile + step, tiles)}, device_id_type=MESH)

    pieces = [stack_ref[r, p].astype(jnp.float32) for r in range(parts) for p in range(sets)]
    fill = outbox.shape[1] - rows
    pieces.append(jnp.zeros((fill, stack_ref.shape[3]), jnp.float32))
    ready = jnp.concatenate(pieces, axis=0).astype(jnp.bfloat16)
    for s in range(strips):
        outbox[s] = ready[:, s * width:(s + 1) * width]

    pl.semaphore_wait(barrier, strips - 1 + tiles - 1)

    asks = []
    for step in range(1, tiles):
        peer = lax.rem(tile + step, tiles)
        copy = pltpu.make_async_remote_copy(
            src_ref=wanted_ref.at[peer], dst_ref=asked.at[step],
            send_sem=ask_sem.at[step], recv_sem=asked_sem.at[step],
            device_id={"tile": peer}, device_id_type=MESH)
        copy.start()
        asks.append(copy)
    sends = []
    for step in range(1, strips):
        peer = lax.rem(me + step, strips)
        copy = pltpu.make_async_remote_copy(
            src_ref=outbox.at[peer], dst_ref=inbox.at[me],
            send_sem=out_sem.at[step], recv_sem=in_sem.at[step],
            device_id={"date": peer // pols, "pol": lax.rem(peer, pols)}, device_id_type=MESH)
        copy.start()
        sends.append(copy)
    inbox[me] = outbox[me]
    fetched_ref[tile] = jnp.zeros(fetched_ref.shape[1:], jnp.bfloat16)
    for copy in sends:
        copy.wait_recv()

    arrived = [inbox[s].astype(jnp.float32) for s in range(strips)]
    pieces = []
    for group in range(parts * sets):
        for s in range(strips):
            pieces.append(arrived[s][group * local:(group + 1) * local])
    table = jnp.concatenate(pieces, axis=0).astype(jnp.bfloat16)
    table_ref[...] = table

    picks = []
    for step in range(1, tiles):
        asks[step - 1].wait_recv()
        asker = lax.rem(tile + tiles - step, tiles)
        chosen = jnp.dot(table, one_hot(asked[step], width), preferred_element_type=jnp.float32)
        picked[step] = chosen.astype(jnp.bfloat16)
        copy = pltpu.make_async_remote_copy(
            src_ref=picked.at[step], dst_ref=fetched_ref.at[tile],
            send_sem=pick_sem.at[step], recv_sem=fetch_sem.at[step],
            device_id={"tile": asker}, device_id_type=MESH)
        copy.start()
        picks.append(copy)
    for copy in picks:
        copy.wait_recv()
    for copy in asks + sends + picks:
        copy.wait_send()


def link_kernel(home_ref, table_ref, fetched_ref, tile_ref, slot_ref, valid_ref, out_ref,
                rows_ref, source_ref, near_ref, gram_re, gram_im):
    features, width = table_ref.shape
    tiles, _, capacity = fetched_ref.shape
    channels = features // 2
    neigh = tile_ref.shape[0]
    chunks = width // LANES
    half = channels // 8
    total = rows_ref.shape[1]

    rows_ref[:, :width] = table_ref[...]
    for q in range(tiles):
        rows_ref[:, width + q * capacity:width + (q + 1) * capacity] = fetched_ref[q]
    owner = tile_ref[...]
    slot = slot_ref[...]
    source_ref[...] = jnp.where(owner == home_ref[0], slot, width + owner * capacity + slot)

    def fetch(k, carry):
        index = source_ref[pl.ds(k, 1), :]
        near = jnp.zeros((features, width), jnp.float32)
        for begin in range(0, total, PIECE):
            size = min(PIECE, total - begin)
            near += jnp.dot(rows_ref[:, begin:begin + size], one_hot(index - begin, size),
                            preferred_element_type=jnp.float32)
        for c in range(chunks):
            near_ref[c, k] = near[:, c * LANES:(c + 1) * LANES]
        return carry

    lax.fori_loop(0, neigh, fetch, 0)

    def link(c, carry):
        lanes = pl.ds(pl.multiple_of(c * LANES, LANES), LANES)
        zero = jnp.zeros((8, LANES), jnp.float32)
        for k in range(neigh):
            mine = [near_ref[c, k, 8 * i:8 * i + 8, :] for i in range(2 * half)]
            for l in range(k, neigh):
                other = [near_ref[c, l, 8 * i:8 * i + 8, :] for i in range(2 * half)]
                real = mine[0] * other[0]
                for i in range(1, 2 * half):
                    real += mine[i] * other[i]
                gram_re[l, 8 * k:8 * k + 8, :] = real
                if l == k:
                    gram_im[l, 8 * k:8 * k + 8, :] = zero
                    continue
                imag = mine[0] * other[half]
                for i in range(1, half):
                    imag += mine[i] * other[half + i]
                back = mine[half] * other[0]
                for i in range(1, half):
                    back += mine[half + i] * other[i]
                imag = imag - back
                gram_re[k, 8 * l:8 * l + 8, :] = real
                gram_im[l, 8 * k:8 * k + 8, :] = imag
                gram_im[k, 8 * l:8 * l + 8, :] = -imag

        def column(ref, l):
            value = ref[l, pl.ds(0, neigh, stride=8), :]
            for j in range(1, 8):
                value += ref[l, pl.ds(j, neigh, stride=8), :]
            return value

        cols_re = [column(gram_re, l) for l in range(neigh)]
        cols_im = [column(gram_im, l) for l in range(neigh)]
        for l in range(neigh):
            gram_re[l, :neigh, :] = cols_re[l]
            gram_im[l, :neigh, :] = cols_im[l]
        mask = valid_ref[:, lanes].astype(jnp.float32)

        u_re = mask * gram_re[0, :neigh, :]
        u_im = mask * gram_im[0, :neigh, :]
        for turn in range(POWER_ITERS - 1):
            g_re = jnp.zeros((neigh, LANES), jnp.float32)
            g_im = jnp.zeros((neigh, LANES), jnp.float32)
            for l in range(neigh):
                a, b = gram_re[l, :neigh, :], gram_im[l, :neigh, :]
                x, y = u_re[l:l + 1, :], u_im[l:l + 1, :]
                g_re += a * x - b * y
                g_im += a * y + b * x
            power = jnp.sum(u_re * g_re + u_im * g_im, axis=0, keepdims=True)
            factor = lax.rsqrt(jnp.maximum(power, 0.0) / channels + eps)
            u_re = mask * g_re * factor
            u_im = mask * g_im * factor

        v_re = jnp.zeros((channels, LANES), jnp.float32)
        v_im = jnp.zeros((channels, LANES), jnp.float32)
        for k in range(neigh):
            a, b = near_ref[c, k, :channels, :], near_ref[c, k, channels:, :]
            x, y = u_re[k:k + 1, :], u_im[k:k + 1, :]
            v_re += a * x - b * y
            v_im += a * y + b * x
        power = jnp.sum(v_re * v_re + v_im * v_im, axis=0, keepdims=True)
        factor = lax.rsqrt(power / channels + eps)
        v_re = v_re * factor
        v_im = v_im * factor
        first_re, first_im = v_re[:1, :], v_im[:1, :]
        denom = jnp.maximum(jnp.sqrt(first_re * first_re + first_im * first_im), floor_value)
        scale_re, scale_im = first_re / denom, first_im / denom
        out_re = v_re * scale_re + v_im * scale_im
        out_im = v_im * scale_re - v_re * scale_im
        dates = out_ref.shape[2]
        for p in range(out_ref.shape[1]):
            out_ref[0, p, :, lanes] = out_re[p * dates:(p + 1) * dates, :]
            out_ref[1, p, :, lanes] = out_im[p * dates:(p + 1) * dates, :]
        return carry

    lax.fori_loop(0, chunks, link, 0)


def body(mesh, stack, nbr_tile, nbr_slot, nbr_valid, fetch_rows):
    dates, pols, tiles = mesh.shape["date"], mesh.shape["pol"], mesh.shape["tile"]
    strips = dates * pols
    parts, local, sets, span = stack.shape
    width = span // strips
    channels = strips * local * sets
    features = parts * channels
    capacity = fetch_rows.shape[-1]
    padded = -(-parts * sets * local // 16) * 16
    vmem = pl.BlockSpec(memory_space=pltpu.VMEM)
    table, fetched = pl.pallas_call(
        functools.partial(gather_kernel, dates, pols, tiles),
        out_shape=(jax.ShapeDtypeStruct((features, width), jnp.bfloat16),
                   jax.ShapeDtypeStruct((tiles, features, capacity), jnp.bfloat16)),
        in_specs=[vmem, vmem],
        out_specs=(vmem, vmem),
        scratch_shapes=[
            pltpu.VMEM((strips, padded, width), jnp.bfloat16),
            pltpu.VMEM((strips, padded, width), jnp.bfloat16),
            pltpu.VMEM((tiles, 1, capacity), jnp.int32),
            pltpu.VMEM((tiles, features, capacity), jnp.bfloat16),
            pltpu.SemaphoreType.DMA((strips,)),
            pltpu.SemaphoreType.DMA((strips,)),
            pltpu.SemaphoreType.DMA((tiles,)),
            pltpu.SemaphoreType.DMA((tiles,)),
            pltpu.SemaphoreType.DMA((tiles,)),
            pltpu.SemaphoreType.DMA((tiles,)),
        ],
        compiler_params=pltpu.CompilerParams(collective_id=0, has_side_effects=True,
                                             vmem_limit_bytes=32 << 20),
        name="gather_rows",
    )(jnp.transpose(stack, (0, 2, 1, 3)), fetch_rows.reshape(tiles, 1, capacity))

    neigh = nbr_tile.shape[0]
    home = lax.axis_index("tile").astype(jnp.int32).reshape(1)
    linked = pl.pallas_call(
        link_kernel,
        out_shape=jax.ShapeDtypeStruct((parts, sets, strips * local, width), jnp.float32),
        in_specs=[pl.BlockSpec(memory_space=pltpu.SMEM)] + [vmem] * 5,
        out_specs=vmem,
        scratch_shapes=[
            pltpu.VMEM((features, width + tiles * capacity), jnp.bfloat16),
            pltpu.VMEM((neigh, width), jnp.int32),
            pltpu.VMEM((width // LANES, neigh, features, LANES), jnp.float32),
            pltpu.VMEM((neigh, 8 * neigh, LANES), jnp.float32),
            pltpu.VMEM((neigh, 8 * neigh, LANES), jnp.float32),
        ],
        compiler_params=pltpu.CompilerParams(vmem_limit_bytes=48 << 20),
        name="link_phases",
    )(home, table, fetched, nbr_tile, nbr_slot, nbr_valid)
    return jnp.transpose(linked, (0, 2, 1, 3))


def solution(mesh):
    in_specs = (
        P(None, ("date", "pol"), None, ("grp", "tile")),
        P(None, ("grp", "tile", "date", "pol")),
        P(None, ("grp", "tile", "date", "pol")),
        P(None, ("grp", "tile", "date", "pol")),
        P(("grp", "tile"), ("date", "pol"), None, None),
    )
    out_specs = P(None, None, None, ("grp", "tile", "date", "pol"))
    return jax.shard_map(functools.partial(body, mesh), mesh=mesh, in_specs=in_specs, out_specs=out_specs,
                         check_vma=False)
```

```python
import functools

import jax
import jax.numpy as jnp
from jax import lax
from jax.experimental import pallas as pl
from jax.experimental.pallas import tpu as pltpu
from jax.sharding import PartitionSpec as P

POWER_ITERS = 8
LANES = 128
PIECE = 256
MESH = pl.DeviceIdType.MESH

eps = 1e-06
floor_value = 0.3


def one_hot(index, rows):
    pieces = []
    for begin in range(0, rows, PIECE):
        size = min(PIECE, rows - begin)
        row = lax.broadcasted_iota(jnp.int32, (size, LANES), 0).astype(jnp.float32).astype(jnp.bfloat16)
        near = (index - begin).astype(jnp.bfloat16)
        one, zero = jnp.ones((size, LANES), jnp.bfloat16), jnp.zeros((size, LANES), jnp.bfloat16)
        pieces.append(jnp.concatenate(
            [jnp.where(row == near[:, c:c + LANES], one, zero) for c in range(0, index.shape[1], LANES)], axis=1))
    return jnp.concatenate(pieces, axis=0)


def phase_kernel(dates, pols, tiles, stack_ref, wanted_ref, tile_ref, slot_ref, valid_ref, out_ref,
                  near_ref, sum_re, sum_im, gram_re, gram_im, last_re, last_im, valid_here, inbox, asked, picked, fetched, table_ref, tile_here, slot_here, source_ref, hot_pick, hot_own, hot_far,
                  own_sem, out_sem, in_sem, ask_sem, asked_sem, pick_sem, fetch_sem):
    strips = dates * pols
    parts, sets, local, _ = stack_ref.shape
    features, width = table_ref.shape
    neigh = tile_ref.shape[0]
    capacity = wanted_ref.shape[-1]
    chunks = width // LANES
    date, pol, tile = lax.axis_index("date"), lax.axis_index("pol"), lax.axis_index("tile")
    me = date * pols + pol

    barrier = pltpu.get_barrier_semaphore()
    for step in range(1, strips):
        peer = lax.rem(me + step, strips)
        pl.semaphore_signal(barrier, inc=1, device_id={"date": peer // pols, "pol": lax.rem(peer, pols)},
                            device_id_type=MESH)
    for step in range(1, tiles):
        pl.semaphore_signal(barrier, inc=1, device_id={"tile": lax.rem(tile + step, tiles)}, device_id_type=MESH)

    def part(strip):
        return stack_ref.at[:, :, :, pl.ds(pl.multiple_of(strip * width, LANES), width)]

    keep = [pltpu.make_async_copy(part(me), inbox.at[me], own_sem.at[0]),
            pltpu.make_async_copy(tile_ref, tile_here, own_sem.at[1]),
            pltpu.make_async_copy(slot_ref, slot_here, own_sem.at[2]),
            pltpu.make_async_copy(valid_ref, valid_here, own_sem.at[3])]
    for copy in keep:
        copy.start()
    fetched[tile] = jnp.zeros(fetched.shape[1:], jnp.bfloat16)

    pl.semaphore_wait(barrier, strips - 1 + tiles - 1)

    asks = []
    for step in range(1, tiles):
        peer = lax.rem(tile + step, tiles)
        copy = pltpu.make_async_remote_copy(
            src_ref=wanted_ref.at[peer], dst_ref=asked.at[step],
            send_sem=ask_sem.at[step], recv_sem=asked_sem.at[step],
            device_id={"tile": peer}, device_id_type=MESH)
        copy.start()
        asks.append(copy)
    sends = []
    for step in range(1, strips):
        peer = lax.rem(me + step, strips)
        copy = pltpu.make_async_remote_copy(
            src_ref=part(peer), dst_ref=inbox.at[me],
            send_sem=out_sem.at[step], recv_sem=in_sem.at[step],
            device_id={"date": peer // pols, "pol": lax.rem(peer, pols)}, device_id_type=MESH)
        copy.start()
        sends.append(copy)

    for copy in keep:
        copy.wait()
    owner, slot = tile_here[...], slot_here[...]
    source_ref[...] = jnp.where(owner == tile, slot, width + owner * capacity + slot).astype(jnp.float32)

    def prepare(k, carry):
        hot_own[k] = one_hot(source_ref[pl.ds(k, 1), :], width)
        return carry

    lax.fori_loop(0, neigh, prepare, 0)
    for step in range(1, tiles):
        asks[step - 1].wait_recv()
        hot_pick[step] = one_hot(asked[step].astype(jnp.float32), width)
    for copy in sends:
        copy.wait_recv()

    pieces = []
    for r in range(parts):
        for p in range(sets):
            for s in range(strips):
                pieces.append(inbox[s, r, p].astype(jnp.float32))
    table_ref[...] = jnp.concatenate(pieces, axis=0).astype(jnp.bfloat16)

    picks = []
    for step in range(1, tiles):
        asker = lax.rem(tile + tiles - step, tiles)
        picked[step] = jnp.dot(table_ref[...], hot_pick[step], preferred_element_type=jnp.float32).astype(jnp.bfloat16)
        copy = pltpu.make_async_remote_copy(
            src_ref=picked.at[step], dst_ref=fetched.at[tile],
            send_sem=pick_sem.at[step], recv_sem=fetch_sem.at[step],
            device_id={"tile": asker}, device_id_type=MESH)
        copy.start()
        picks.append(copy)

    far = tiles * capacity
    early = hot_far.shape[1] == far

    def gather_own(k, carry):
        if early:
            hot_far[k] = one_hot(source_ref[pl.ds(k, 1), :] - width, far)
        near = jnp.dot(table_ref[...], hot_own[k], preferred_element_type=jnp.float32)
        for c in range(chunks):
            near_ref[c, k] = near[:, c * LANES:(c + 1) * LANES]
        return carry

    lax.fori_loop(0, neigh, gather_own, 0)
    for copy in picks:
        copy.wait_recv()

    def gather_far(k, carry):
        group = max(1, 2 * PIECE // capacity)
        near = jnp.zeros((features, width), jnp.float32)
        for begin in range(0, tiles, group):
            end = min(tiles, begin + group)
            rows = jnp.concatenate([fetched[q] for q in range(begin, end)], axis=1)
            first, size = begin * capacity, (end - begin) * capacity
            if early:
                hot = hot_far[k, first:first + size, :]
            else:
                hot = one_hot(source_ref[pl.ds(k, 1), :] - (width + first), size)
            near += jnp.dot(rows, hot, preferred_element_type=jnp.float32)
        for c in range(chunks):
            near_ref[c, k] += near[:, c * LANES:(c + 1) * LANES]
        return carry

    group = next(n for n in (4, 4, 2, 1) if neigh % n == 0)

    def gather_group(i, carry):
        for j in range(group):
            carry = gather_far(i * group + j, carry)
        return carry

    lax.fori_loop(0, neigh // group, gather_group, 0)
    link_rows(near_ref, valid_here, out_ref, sum_re, sum_im, gram_re, gram_im, last_re, last_im)
    for copy in asks + sends + picks:
        copy.wait_send()


def link_rows(near_ref, valid_ref, out_ref, sum_re, sum_im, gram_re, gram_im, last_re, last_im):
    chunks, neigh, features, _ = near_ref.shape
    channels = features // 2
    half = channels // 8

    def pairs(c, carry):
        lanes = pl.ds(pl.multiple_of(c * LANES, LANES), LANES)
        zero = jnp.zeros((8, LANES), jnp.float32)
        for k in range(neigh):
            mine = [near_ref[c, k, 8 * i:8 * i + 8, :] for i in range(2 * half)]
            for l in range(k, neigh):
                other = [near_ref[c, l, 8 * i:8 * i + 8, :] for i in range(2 * half)]
                real = mine[0] * other[0]
                for i in range(1, 2 * half):
                    real += mine[i] * other[i]
                sum_re[l, 8 * k:8 * k + 8, :] = real
                if l == k:
                    sum_im[l, 8 * k:8 * k + 8, :] = zero
                    continue
                imag = mine[0] * other[half]
                for i in range(1, half):
                    imag += mine[i] * other[half + i]
                back = mine[half] * other[0]
                for i in range(1, half):
                    back += mine[half + i] * other[i]
                imag = imag - back
                sum_re[k, 8 * l:8 * l + 8, :] = real
                sum_im[l, 8 * k:8 * k + 8, :] = imag
                sum_im[k, 8 * l:8 * l + 8, :] = -imag
        for l in range(neigh):
            for held, gram in ((sum_re, gram_re), (sum_im, gram_im)):
                value = held[l, pl.ds(0, neigh, stride=8), :]
                for j in range(1, 8):
                    value += held[l, pl.ds(j, neigh, stride=8), :]
                gram[l, :, lanes] = value
        return carry

    lax.fori_loop(0, chunks, pairs, 0)

    mask = valid_ref[...].astype(jnp.float32)
    u_re = mask * gram_re[0]
    u_im = mask * gram_im[0]
    for turn in range(POWER_ITERS - 1):
        g_re = jnp.zeros(mask.shape, jnp.float32)
        g_im = jnp.zeros(mask.shape, jnp.float32)
        for l in range(neigh):
            a, b = gram_re[l], gram_im[l]
            x, y = u_re[l:l + 1, :], u_im[l:l + 1, :]
            g_re += a * x - b * y
            g_im += a * y + b * x
        power = jnp.sum(u_re * g_re + u_im * g_im, axis=0, keepdims=True)
        factor = lax.rsqrt(jnp.maximum(power, 0.0) / channels + eps)
        u_re = mask * g_re * factor
        u_im = mask * g_im * factor
    last_re[...] = u_re
    last_im[...] = u_im

    dates = out_ref.shape[2]
    for c in range(chunks):
        lanes = slice(c * LANES, (c + 1) * LANES)
        v_re = jnp.zeros((channels, LANES), jnp.float32)
        v_im = jnp.zeros((channels, LANES), jnp.float32)
        for k in range(neigh):
            a, b = near_ref[c, k, :channels, :], near_ref[c, k, channels:, :]
            x, y = last_re[k:k + 1, lanes], last_im[k:k + 1, lanes]
            v_re += a * x - b * y
            v_im += a * y + b * x
        power = jnp.sum(v_re * v_re + v_im * v_im, axis=0, keepdims=True)
        factor = lax.rsqrt(power / channels + eps)
        v_re = v_re * factor
        v_im = v_im * factor
        first_re, first_im = v_re[:1, :], v_im[:1, :]
        denom = jnp.maximum(jnp.sqrt(first_re * first_re + first_im * first_im), floor_value)
        scale_re, scale_im = first_re / denom, first_im / denom
        out_re = v_re * scale_re + v_im * scale_im
        out_im = v_im * scale_re - v_re * scale_im
        for p in range(out_ref.shape[1]):
            out_ref[0, p, :, lanes] = out_re[p * dates:(p + 1) * dates, :]
            out_ref[1, p, :, lanes] = out_im[p * dates:(p + 1) * dates, :]


def body(mesh, stack, nbr_tile, nbr_slot, nbr_valid, fetch_rows):
    dates, pols, tiles = mesh.shape["date"], mesh.shape["pol"], mesh.shape["tile"]
    strips = dates * pols
    parts, local, sets, span = stack.shape
    width = span // strips
    features = parts * strips * local * sets
    capacity = fetch_rows.shape[-1]
    neigh = nbr_tile.shape[0]
    far = tiles * capacity if tiles * capacity <= 1024 else 16
    vmem = pl.BlockSpec(memory_space=pltpu.VMEM)
    anywhere = pl.BlockSpec(memory_space=pl.ANY)
    linked = pl.pallas_call(
        functools.partial(phase_kernel, dates, pols, tiles),
        out_shape=jax.ShapeDtypeStruct((parts, sets, strips * local, width), jnp.float32),
        in_specs=[anywhere] * 5,
        out_specs=vmem,
        scratch_shapes=[
            pltpu.VMEM((width // LANES, neigh, features, LANES), jnp.float32),
            pltpu.VMEM((neigh, 8 * neigh, LANES), jnp.float32),
            pltpu.VMEM((neigh, 8 * neigh, LANES), jnp.float32),
            pltpu.VMEM((neigh, neigh, width), jnp.float32),
            pltpu.VMEM((neigh, neigh, width), jnp.float32),
            pltpu.VMEM((neigh, width), jnp.float32),
            pltpu.VMEM((neigh, width), jnp.float32),
            pltpu.VMEM((neigh, width), jnp.int32),
            pltpu.VMEM((strips, parts, sets, local, width), jnp.bfloat16),
            pltpu.VMEM((tiles, 1, capacity), jnp.int32),
            pltpu.VMEM((tiles, features, capacity), jnp.bfloat16),
            pltpu.VMEM((tiles, features, capacity), jnp.bfloat16),
            pltpu.VMEM((features, width), jnp.bfloat16),
            pltpu.VMEM((neigh, width), jnp.int32),
            pltpu.VMEM((neigh, width), jnp.int32),
            pltpu.VMEM((neigh, width), jnp.float32),
            pltpu.VMEM((tiles, width, capacity), jnp.bfloat16),
            pltpu.VMEM((neigh, width, width), jnp.bfloat16),
            pltpu.VMEM((neigh, far, width), jnp.bfloat16),
            pltpu.SemaphoreType.DMA((4,)),
            pltpu.SemaphoreType.DMA((strips,)),
            pltpu.SemaphoreType.DMA((strips,)),
            pltpu.SemaphoreType.DMA((tiles,)),
            pltpu.SemaphoreType.DMA((tiles,)),
            pltpu.SemaphoreType.DMA((tiles,)),
            pltpu.SemaphoreType.DMA((tiles,)),
        ],
        compiler_params=pltpu.CompilerParams(collective_id=0, has_side_effects=True,
                                             vmem_limit_bytes=60 << 20),
        name="phase_rows",
    )(jnp.transpose(stack, (0, 2, 1, 3)), fetch_rows.reshape(tiles, 1, capacity), nbr_tile, nbr_slot, nbr_valid)

    return jnp.transpose(linked, (0, 2, 1, 3))


def solution(mesh):
    in_specs = (
        P(None, ("date", "pol"), None, ("grp", "tile")),
        P(None, ("grp", "tile", "date", "pol")),
        P(None, ("grp", "tile", "date", "pol")),
        P(None, ("grp", "tile", "date", "pol")),
        P(("grp", "tile"), ("date", "pol"), None, None),
    )
    out_specs = P(None, None, None, ("grp", "tile", "date", "pol"))
    return jax.shard_map(functools.partial(body, mesh), mesh=mesh, in_specs=in_specs, out_specs=out_specs,
                         check_vma=False)
```

```python
import functools

import jax
import jax.numpy as jnp
from jax import lax
from jax.experimental import pallas as pl
from jax.experimental.pallas import tpu as pltpu
from jax.sharding import PartitionSpec as P

POWER_ITERS = 8
LANES = 128
PIECE = 256
MESH = pl.DeviceIdType.MESH

eps = 1e-06
floor_value = 0.3


def one_hot(index, rows):
    pieces = []
    for begin in range(0, rows, PIECE):
        size = min(PIECE, rows - begin)
        row = lax.broadcasted_iota(jnp.int32, (size, LANES), 0).astype(jnp.float32).astype(jnp.bfloat16)
        near = (index - begin).astype(jnp.bfloat16)
        one, zero = jnp.ones((size, LANES), jnp.bfloat16), jnp.zeros((size, LANES), jnp.bfloat16)
        pieces.append(jnp.concatenate(
            [jnp.where(row == near[:, c:c + LANES], one, zero) for c in range(0, index.shape[1], LANES)], axis=1))
    return jnp.concatenate(pieces, axis=0)


def phase_kernel(dates, pols, tiles, stack_ref, wanted_ref, tile_ref, slot_ref, valid_ref, out_ref,
                  near_ref, diff_ref, sum_re, sum_im, gram_re, gram_im, last_re, last_im, valid_here, inbox, asked, picked, fetched, table_ref, tile_here, slot_here, source_ref, hot_pick, hot_own, hot_far,
                  own_sem, out_sem, in_sem, ask_sem, asked_sem, pick_sem, fetch_sem):
    strips = dates * pols
    parts, sets, local, _ = stack_ref.shape
    features, width = table_ref.shape
    neigh = tile_ref.shape[0]
    capacity = wanted_ref.shape[-1]
    chunks = width // LANES
    date, pol, tile = lax.axis_index("date"), lax.axis_index("pol"), lax.axis_index("tile")
    me = date * pols + pol

    barrier = pltpu.get_barrier_semaphore()
    for step in range(1, strips):
        peer = lax.rem(me + step, strips)
        pl.semaphore_signal(barrier, inc=1, device_id={"date": peer // pols, "pol": lax.rem(peer, pols)},
                            device_id_type=MESH)
    for step in range(1, tiles):
        pl.semaphore_signal(barrier, inc=1, device_id={"tile": lax.rem(tile + step, tiles)}, device_id_type=MESH)

    def part(strip):
        return stack_ref.at[:, :, :, pl.ds(pl.multiple_of(strip * width, LANES), width)]

    keep = [pltpu.make_async_copy(part(me), inbox.at[me], own_sem.at[0]),
            pltpu.make_async_copy(tile_ref, tile_here, own_sem.at[1]),
            pltpu.make_async_copy(slot_ref, slot_here, own_sem.at[2]),
            pltpu.make_async_copy(valid_ref, valid_here, own_sem.at[3])]
    for copy in keep:
        copy.start()
    fetched[tile] = jnp.zeros(fetched.shape[1:], jnp.bfloat16)

    pl.semaphore_wait(barrier, strips - 1 + tiles - 1)

    asks = []
    for step in range(1, tiles):
        peer = lax.rem(tile + step, tiles)
        copy = pltpu.make_async_remote_copy(
            src_ref=wanted_ref.at[peer], dst_ref=asked.at[step],
            send_sem=ask_sem.at[step], recv_sem=asked_sem.at[step],
            device_id={"tile": peer}, device_id_type=MESH)
        copy.start()
        asks.append(copy)
    sends = []
    for step in range(1, strips):
        peer = lax.rem(me + step, strips)
        copy = pltpu.make_async_remote_copy(
            src_ref=part(peer), dst_ref=inbox.at[me],
            send_sem=out_sem.at[step], recv_sem=in_sem.at[step],
            device_id={"date": peer // pols, "pol": lax.rem(peer, pols)}, device_id_type=MESH)
        copy.start()
        sends.append(copy)

    for copy in keep:
        copy.wait()
    owner, slot = tile_here[...], slot_here[...]
    source_ref[...] = jnp.where(owner == tile, slot, width + owner * capacity + slot).astype(jnp.float32)

    def prepare(k, carry):
        hot_own[k] = one_hot(source_ref[pl.ds(k, 1), :], width)
        return carry

    lax.fori_loop(0, neigh, prepare, 0)
    for step in range(1, tiles):
        asks[step - 1].wait_recv()
        hot_pick[step] = one_hot(asked[step].astype(jnp.float32), width)
    for copy in sends:
        copy.wait_recv()

    pieces = []
    for r in range(parts):
        for p in range(sets):
            for s in range(strips):
                pieces.append(inbox[s, r, p].astype(jnp.float32))
    table_ref[...] = jnp.concatenate(pieces, axis=0).astype(jnp.bfloat16)

    for step in range(1, tiles):
        picked[step] = jnp.dot(table_ref[...], hot_pick[step], preferred_element_type=jnp.float32).astype(jnp.bfloat16)
    picks = []
    for step in range(1, tiles):
        asker = lax.rem(tile + tiles - step, tiles)
        copy = pltpu.make_async_remote_copy(
            src_ref=picked.at[step], dst_ref=fetched.at[tile],
            send_sem=pick_sem.at[step], recv_sem=fetch_sem.at[step],
            device_id={"tile": asker}, device_id_type=MESH)
        copy.start()
        picks.append(copy)

    far = tiles * capacity
    early = hot_far.shape[1] == far

    def gather_own(k, carry):
        if early:
            hot_far[k] = one_hot(source_ref[pl.ds(k, 1), :] - width, far)
        near = jnp.dot(table_ref[...], hot_own[k], preferred_element_type=jnp.float32)
        for c in range(chunks):
            near_ref[c, k] = near[:, c * LANES:(c + 1) * LANES]
        return carry

    group = next(n for n in (4, 2, 1) if neigh % n == 0)

    def own_group(i, carry):
        for j in range(group):
            carry = gather_own(i * group + j, carry)
        return carry

    lax.fori_loop(0, neigh // group, own_group, 0)
    for copy in picks:
        copy.wait_recv()

    def gather_far(k, carry):
        group = max(1, 2 * PIECE // capacity)
        near = jnp.zeros((features, width), jnp.float32)
        for begin in range(0, tiles, group):
            end = min(tiles, begin + group)
            block = jnp.concatenate([fetched[q] for q in range(begin, end)], axis=1)
            first, size = begin * capacity, (end - begin) * capacity
            if early:
                hot = hot_far[k, first:first + size, :]
            else:
                hot = one_hot(source_ref[pl.ds(k, 1), :] - (width + first), size)
            near += jnp.dot(block, hot, preferred_element_type=jnp.float32)
        for c in range(chunks):
            rows = near_ref[c, k] + near[:, c * LANES:(c + 1) * LANES]
            near_ref[c, k] = rows
            diff_ref[c, k] = rows[:features // 2] - rows[features // 2:]
        return carry

    def gather_group(i, carry):
        for j in range(group):
            carry = gather_far(i * group + j, carry)
        return carry

    lax.fori_loop(0, neigh // group, gather_group, 0)
    link_rows(near_ref, diff_ref, valid_here, out_ref, sum_re, sum_im, gram_re, gram_im, last_re, last_im)
    for copy in asks + sends + picks:
        copy.wait_send()


def link_rows(near_ref, diff_ref, valid_ref, out_ref, sum_re, sum_im, gram_re, gram_im, last_re, last_im):
    chunks, neigh, features, _ = near_ref.shape
    channels = features // 2
    half = channels // 8

    def pairs(c, carry):
        lanes = pl.ds(pl.multiple_of(c * LANES, LANES), LANES)
        zero = jnp.zeros((8, LANES), jnp.float32)
        for k in range(neigh):
            mine = [near_ref[c, k, 8 * i:8 * i + 8, :] for i in range(2 * half)]
            both = [mine[i] + mine[half + i] for i in range(half)]
            for l in range(k, neigh):
                other = [near_ref[c, l, 8 * i:8 * i + 8, :] for i in range(2 * half)]
                first = mine[0] * other[0]
                second = mine[half] * other[half]
                for i in range(1, half):
                    first += mine[i] * other[i]
                    second += mine[half + i] * other[half + i]
                real = first + second
                sum_re[l, 8 * k:8 * k + 8, :] = real
                if l == k:
                    sum_im[l, 8 * k:8 * k + 8, :] = zero
                    continue
                third = both[0] * diff_ref[c, l, :8, :]
                for i in range(1, half):
                    third += both[i] * diff_ref[c, l, 8 * i:8 * i + 8, :]
                imag = first - second - third
                sum_re[k, 8 * l:8 * l + 8, :] = real
                sum_im[l, 8 * k:8 * k + 8, :] = imag
                sum_im[k, 8 * l:8 * l + 8, :] = -imag
        for l in range(neigh):
            for held, gram in ((sum_re, gram_re), (sum_im, gram_im)):
                value = held[l, pl.ds(0, neigh, stride=8), :]
                for j in range(1, 8):
                    value += held[l, pl.ds(j, neigh, stride=8), :]
                gram[l, :, lanes] = value
        return carry

    lax.fori_loop(0, chunks, pairs, 0)

    mask = valid_ref[...].astype(jnp.float32)
    u_re = mask * gram_re[0]
    u_im = mask * gram_im[0]
    for turn in range(POWER_ITERS - 1):
        g_re = jnp.zeros(mask.shape, jnp.float32)
        g_im = jnp.zeros(mask.shape, jnp.float32)
        for l in range(neigh):
            a, b = gram_re[l], gram_im[l]
            x, y = u_re[l:l + 1, :], u_im[l:l + 1, :]
            g_re += a * x - b * y
            g_im += a * y + b * x
        power = jnp.sum(u_re * g_re + u_im * g_im, axis=0, keepdims=True)
        factor = lax.rsqrt(jnp.maximum(power, 0.0) / channels + eps)
        u_re = mask * g_re * factor
        u_im = mask * g_im * factor
    last_re[...] = u_re
    last_im[...] = u_im

    dates = out_ref.shape[2]
    for c in range(chunks):
        lanes = slice(c * LANES, (c + 1) * LANES)
        v_re = jnp.zeros((channels, LANES), jnp.float32)
        v_im = jnp.zeros((channels, LANES), jnp.float32)
        for k in range(neigh):
            a, b = near_ref[c, k, :channels, :], near_ref[c, k, channels:, :]
            x, y = last_re[k:k + 1, lanes], last_im[k:k + 1, lanes]
            v_re += a * x - b * y
            v_im += a * y + b * x
        power = jnp.sum(v_re * v_re + v_im * v_im, axis=0, keepdims=True)
        factor = lax.rsqrt(power / channels + eps)
        v_re = v_re * factor
        v_im = v_im * factor
        first_re, first_im = v_re[:1, :], v_im[:1, :]
        denom = jnp.maximum(jnp.sqrt(first_re * first_re + first_im * first_im), floor_value)
        scale_re, scale_im = first_re / denom, first_im / denom
        out_re = v_re * scale_re + v_im * scale_im
        out_im = v_im * scale_re - v_re * scale_im
        for p in range(out_ref.shape[1]):
            out_ref[0, p, :, lanes] = out_re[p * dates:(p + 1) * dates, :]
            out_ref[1, p, :, lanes] = out_im[p * dates:(p + 1) * dates, :]


def body(mesh, stack, nbr_tile, nbr_slot, nbr_valid, fetch_rows):
    dates, pols, tiles = mesh.shape["date"], mesh.shape["pol"], mesh.shape["tile"]
    strips = dates * pols
    parts, local, sets, span = stack.shape
    width = span // strips
    features = parts * strips * local * sets
    capacity = fetch_rows.shape[-1]
    neigh = nbr_tile.shape[0]
    far = tiles * capacity if tiles * capacity <= 1024 else 16
    vmem = pl.BlockSpec(memory_space=pltpu.VMEM)
    anywhere = pl.BlockSpec(memory_space=pl.ANY)
    linked = pl.pallas_call(
        functools.partial(phase_kernel, dates, pols, tiles),
        out_shape=jax.ShapeDtypeStruct((parts, sets, strips * local, width), jnp.float32),
        in_specs=[anywhere] * 5,
        out_specs=vmem,
        scratch_shapes=[
            pltpu.VMEM((width // LANES, neigh, features, LANES), jnp.float32),
            pltpu.VMEM((width // LANES, neigh, features // 2, LANES), jnp.float32),
            pltpu.VMEM((neigh, 8 * neigh, LANES), jnp.float32),
            pltpu.VMEM((neigh, 8 * neigh, LANES), jnp.float32),
            pltpu.VMEM((neigh, neigh, width), jnp.float32),
            pltpu.VMEM((neigh, neigh, width), jnp.float32),
            pltpu.VMEM((neigh, width), jnp.float32),
            pltpu.VMEM((neigh, width), jnp.float32),
            pltpu.VMEM((neigh, width), jnp.int32),
            pltpu.VMEM((strips, parts, sets, local, width), jnp.bfloat16),
            pltpu.VMEM((tiles, 1, capacity), jnp.int32),
            pltpu.VMEM((tiles, features, capacity), jnp.bfloat16),
            pltpu.VMEM((tiles, features, capacity), jnp.bfloat16),
            pltpu.VMEM((features, width), jnp.bfloat16),
            pltpu.VMEM((neigh, width), jnp.int32),
            pltpu.VMEM((neigh, width), jnp.int32),
            pltpu.VMEM((neigh, width), jnp.float32),
            pltpu.VMEM((tiles, width, capacity), jnp.bfloat16),
            pltpu.VMEM((neigh, width, width), jnp.bfloat16),
            pltpu.VMEM((neigh, far, width), jnp.bfloat16),
            pltpu.SemaphoreType.DMA((4,)),
            pltpu.SemaphoreType.DMA((strips,)),
            pltpu.SemaphoreType.DMA((strips,)),
            pltpu.SemaphoreType.DMA((tiles,)),
            pltpu.SemaphoreType.DMA((tiles,)),
            pltpu.SemaphoreType.DMA((tiles,)),
            pltpu.SemaphoreType.DMA((tiles,)),
        ],
        compiler_params=pltpu.CompilerParams(collective_id=0, has_side_effects=True,
                                             vmem_limit_bytes=60 << 20),
        name="phase_rows",
    )(jnp.transpose(stack, (0, 2, 1, 3)), fetch_rows.reshape(tiles, 1, capacity), nbr_tile, nbr_slot, nbr_valid)

    return jnp.transpose(linked, (0, 2, 1, 3))


def solution(mesh):
    in_specs = (
        P(None, ("date", "pol"), None, ("grp", "tile")),
        P(None, ("grp", "tile", "date", "pol")),
        P(None, ("grp", "tile", "date", "pol")),
        P(None, ("grp", "tile", "date", "pol")),
        P(("grp", "tile"), ("date", "pol"), None, None),
    )
    out_specs = P(None, None, None, ("grp", "tile", "date", "pol"))
    return jax.shard_map(functools.partial(body, mesh), mesh=mesh, in_specs=in_specs, out_specs=out_specs,
                         check_vma=False)
```

```python
import functools

import jax
import jax.numpy as jnp
from jax import lax
from jax.experimental import pallas as pl
from jax.experimental.pallas import tpu as pltpu
from jax.sharding import PartitionSpec as P

POWER_ITERS = 8
LANES = 128
PIECE = 256
MESH = pl.DeviceIdType.MESH

eps = 1e-06
floor_value = 0.3


def one_hot(index, rows):
    pieces = []
    for begin in range(0, rows, PIECE):
        size = min(PIECE, rows - begin)
        row = lax.broadcasted_iota(jnp.int32, (size, LANES), 0).astype(jnp.float32).astype(jnp.bfloat16)
        near = (index - begin).astype(jnp.bfloat16)
        one, zero = jnp.ones((size, LANES), jnp.bfloat16), jnp.zeros((size, LANES), jnp.bfloat16)
        pieces.append(jnp.concatenate(
            [jnp.where(row == near[:, c:c + LANES], one, zero) for c in range(0, index.shape[1], LANES)], axis=1))
    return jnp.concatenate(pieces, axis=0)


def phase_kernel(dates, pols, tiles, stack_ref, wanted_ref, tile_ref, slot_ref, valid_ref, out_ref,
                  near_ref, diff_ref, sum_re, sum_im, gram_re, gram_im, last_re, last_im, valid_here, inbox, asked, picked, fetched, table_ref, tile_here, slot_here, source_ref, hot_pick, hot_own, hot_far,
                  own_sem, out_sem, in_sem, ask_sem, asked_sem, pick_sem, fetch_sem):
    strips = dates * pols
    parts, sets, local, _ = stack_ref.shape
    features, width = table_ref.shape
    neigh = tile_ref.shape[0]
    capacity = wanted_ref.shape[-1]
    chunks = width // LANES
    date, pol, tile = lax.axis_index("date"), lax.axis_index("pol"), lax.axis_index("tile")
    me = date * pols + pol

    barrier = pltpu.get_barrier_semaphore()
    for step in range(1, strips):
        peer = lax.rem(me + step, strips)
        pl.semaphore_signal(barrier, inc=1, device_id={"date": peer // pols, "pol": lax.rem(peer, pols)},
                            device_id_type=MESH)
    for step in range(1, tiles):
        pl.semaphore_signal(barrier, inc=1, device_id={"tile": lax.rem(tile + step, tiles)}, device_id_type=MESH)

    def part(strip):
        return stack_ref.at[:, :, :, pl.ds(pl.multiple_of(strip * width, LANES), width)]

    keep = [pltpu.make_async_copy(part(me), inbox.at[me], own_sem.at[0]),
            pltpu.make_async_copy(tile_ref, tile_here, own_sem.at[1]),
            pltpu.make_async_copy(slot_ref, slot_here, own_sem.at[2]),
            pltpu.make_async_copy(valid_ref, valid_here, own_sem.at[3])]
    for copy in keep:
        copy.start()
    fetched[tile] = jnp.zeros(fetched.shape[1:], jnp.bfloat16)

    pl.semaphore_wait(barrier, strips - 1 + tiles - 1)

    sends = []
    for step in range(1, strips):
        peer = lax.rem(me + step, strips)
        copy = pltpu.make_async_remote_copy(
            src_ref=part(peer), dst_ref=inbox.at[me],
            send_sem=out_sem.at[step], recv_sem=in_sem.at[step],
            device_id={"date": peer // pols, "pol": lax.rem(peer, pols)}, device_id_type=MESH)
        copy.start()
        sends.append(copy)
    asks = []
    for step in range(1, tiles):
        peer = lax.rem(tile + step, tiles)
        copy = pltpu.make_async_remote_copy(
            src_ref=wanted_ref.at[peer], dst_ref=asked.at[step],
            send_sem=ask_sem.at[step], recv_sem=asked_sem.at[step],
            device_id={"tile": peer}, device_id_type=MESH)
        copy.start()
        asks.append(copy)
    for copy in keep:
        copy.wait()
    owner, slot = tile_here[...], slot_here[...]
    source_ref[...] = jnp.where(owner == tile, slot, width + owner * capacity + slot).astype(jnp.float32)

    def prepare(k, carry):
        hot_own[k] = one_hot(source_ref[pl.ds(k, 1), :], width)
        return carry

    lax.fori_loop(0, neigh, prepare, 0)
    for step in range(1, tiles):
        asks[step - 1].wait_recv()
        hot_pick[step] = one_hot(asked[step].astype(jnp.float32), width)
    for copy in sends:
        copy.wait_recv()

    pieces = []
    for r in range(parts):
        for p in range(sets):
            for s in range(strips):
                pieces.append(inbox[s, r, p].astype(jnp.float32))
    table_ref[...] = jnp.concatenate(pieces, axis=0).astype(jnp.bfloat16)

    for step in range(1, tiles):
        picked[step] = jnp.dot(table_ref[...], hot_pick[step], preferred_element_type=jnp.float32).astype(jnp.bfloat16)
    picks = []
    for step in range(1, tiles):
        asker = lax.rem(tile + tiles - step, tiles)
        copy = pltpu.make_async_remote_copy(
            src_ref=picked.at[step], dst_ref=fetched.at[tile],
            send_sem=pick_sem.at[step], recv_sem=fetch_sem.at[step],
            device_id={"tile": asker}, device_id_type=MESH)
        copy.start()
        picks.append(copy)

    far = tiles * capacity
    early = hot_far.shape[1] == far

    def gather_own(k, carry):
        if early:
            hot_far[k] = one_hot(source_ref[pl.ds(k, 1), :] - width, far)
        near = jnp.dot(table_ref[...], hot_own[k], preferred_element_type=jnp.float32)
        for c in range(chunks):
            near_ref[c, k] = near[:, c * LANES:(c + 1) * LANES]
        return carry

    group = next(n for n in (8, 4, 2, 1) if neigh % n == 0)

    def own_group(i, carry):
        for j in range(group):
            carry = gather_own(i * group + j, carry)
        return carry

    lax.fori_loop(0, neigh // group, own_group, 0)
    for copy in picks:
        copy.wait_recv()

    def gather_far(k, carry):
        group = max(1, 2 * PIECE // capacity)
        near = jnp.zeros((features, width), jnp.float32)
        for begin in range(0, tiles, group):
            end = min(tiles, begin + group)
            block = jnp.concatenate([fetched[q] for q in range(begin, end)], axis=1)
            first, size = begin * capacity, (end - begin) * capacity
            if early:
                hot = hot_far[k, first:first + size, :]
            else:
                hot = one_hot(source_ref[pl.ds(k, 1), :] - (width + first), size)
            near += jnp.dot(block, hot, preferred_element_type=jnp.float32)
        for c in range(chunks):
            rows = near_ref[c, k] + near[:, c * LANES:(c + 1) * LANES]
            near_ref[c, k] = rows
            diff_ref[c, k] = rows[:features // 2] - rows[features // 2:]
        return carry

    def gather_group(i, carry):
        for j in range(group):
            carry = gather_far(i * group + j, carry)
        return carry

    lax.fori_loop(0, neigh // group, gather_group, 0)
    link_rows(near_ref, diff_ref, valid_here, out_ref, sum_re, sum_im, gram_re, gram_im, last_re, last_im)
    for copy in asks + sends + picks:
        copy.wait_send()


def link_rows(near_ref, diff_ref, valid_ref, out_ref, sum_re, sum_im, gram_re, gram_im, last_re, last_im):
    chunks, neigh, features, _ = near_ref.shape
    channels = features // 2
    half = channels // 8

    def pairs(c, carry):
        lanes = pl.ds(pl.multiple_of(c * LANES, LANES), LANES)
        zero = jnp.zeros((8, LANES), jnp.float32)
        for k in range(neigh):
            mine = [near_ref[c, k, 8 * i:8 * i + 8, :] for i in range(2 * half)]
            both = [mine[i] + mine[half + i] for i in range(half)]
            for l in range(k, neigh):
                other = [near_ref[c, l, 8 * i:8 * i + 8, :] for i in range(2 * half)]
                first = mine[0] * other[0]
                second = mine[half] * other[half]
                for i in range(1, half):
                    first += mine[i] * other[i]
                    second += mine[half + i] * other[half + i]
                real = first + second
                sum_re[l, 8 * k:8 * k + 8, :] = real
                if l == k:
                    sum_im[l, 8 * k:8 * k + 8, :] = zero
                    continue
                third = both[0] * diff_ref[c, l, :8, :]
                for i in range(1, half):
                    third += both[i] * diff_ref[c, l, 8 * i:8 * i + 8, :]
                imag = first - second - third
                sum_re[k, 8 * l:8 * l + 8, :] = real
                sum_im[l, 8 * k:8 * k + 8, :] = imag
                sum_im[k, 8 * l:8 * l + 8, :] = -imag
        for l in range(neigh):
            for held, gram in ((sum_re, gram_re), (sum_im, gram_im)):
                value = held[l, pl.ds(0, neigh, stride=8), :]
                for j in range(1, 8):
                    value += held[l, pl.ds(j, neigh, stride=8), :]
                gram[l, :, lanes] = value
        return carry

    lax.fori_loop(0, chunks, pairs, 0)

    mask = valid_ref[...].astype(jnp.float32)
    u_re = mask * gram_re[0]
    u_im = mask * gram_im[0]
    for turn in range(POWER_ITERS - 1):
        g_re = jnp.zeros(mask.shape, jnp.float32)
        g_im = jnp.zeros(mask.shape, jnp.float32)
        for l in range(neigh):
            a, b = gram_re[l], gram_im[l]
            x, y = u_re[l:l + 1, :], u_im[l:l + 1, :]
            g_re += a * x - b * y
            g_im += a * y + b * x
        power = jnp.sum(u_re * g_re + u_im * g_im, axis=0, keepdims=True)
        factor = lax.rsqrt(jnp.maximum(power, 0.0) / channels + eps)
        u_re = mask * g_re * factor
        u_im = mask * g_im * factor
    last_re[...] = u_re
    last_im[...] = u_im

    dates = out_ref.shape[2]
    for c in range(chunks):
        lanes = slice(c * LANES, (c + 1) * LANES)
        v_re = jnp.zeros((channels, LANES), jnp.float32)
        v_im = jnp.zeros((channels, LANES), jnp.float32)
        for k in range(neigh):
            a, b = near_ref[c, k, :channels, :], near_ref[c, k, channels:, :]
            x, y = last_re[k:k + 1, lanes], last_im[k:k + 1, lanes]
            v_re += a * x - b * y
            v_im += a * y + b * x
        power = jnp.sum(v_re * v_re + v_im * v_im, axis=0, keepdims=True)
        factor = lax.rsqrt(power / channels + eps)
        v_re = v_re * factor
        v_im = v_im * factor
        first_re, first_im = v_re[:1, :], v_im[:1, :]
        denom = jnp.maximum(jnp.sqrt(first_re * first_re + first_im * first_im), floor_value)
        scale_re, scale_im = first_re / denom, first_im / denom
        out_re = v_re * scale_re + v_im * scale_im
        out_im = v_im * scale_re - v_re * scale_im
        for p in range(out_ref.shape[1]):
            out_ref[0, p, :, lanes] = out_re[p * dates:(p + 1) * dates, :]
            out_ref[1, p, :, lanes] = out_im[p * dates:(p + 1) * dates, :]


def body(mesh, stack, nbr_tile, nbr_slot, nbr_valid, fetch_rows):
    dates, pols, tiles = mesh.shape["date"], mesh.shape["pol"], mesh.shape["tile"]
    strips = dates * pols
    parts, local, sets, span = stack.shape
    width = span // strips
    features = parts * strips * local * sets
    capacity = fetch_rows.shape[-1]
    neigh = nbr_tile.shape[0]
    far = tiles * capacity if tiles * capacity <= 1024 else 16
    vmem = pl.BlockSpec(memory_space=pltpu.VMEM)
    anywhere = pl.BlockSpec(memory_space=pl.ANY)
    linked = pl.pallas_call(
        functools.partial(phase_kernel, dates, pols, tiles),
        out_shape=jax.ShapeDtypeStruct((parts, sets, strips * local, width), jnp.float32),
        in_specs=[anywhere] * 5,
        out_specs=vmem,
        scratch_shapes=[
            pltpu.VMEM((width // LANES, neigh, features, LANES), jnp.float32),
            pltpu.VMEM((width // LANES, neigh, features // 2, LANES), jnp.float32),
            pltpu.VMEM((neigh, 8 * neigh, LANES), jnp.float32),
            pltpu.VMEM((neigh, 8 * neigh, LANES), jnp.float32),
            pltpu.VMEM((neigh, neigh, width), jnp.float32),
            pltpu.VMEM((neigh, neigh, width), jnp.float32),
            pltpu.VMEM((neigh, width), jnp.float32),
            pltpu.VMEM((neigh, width), jnp.float32),
            pltpu.VMEM((neigh, width), jnp.int32),
            pltpu.VMEM((strips, parts, sets, local, width), jnp.bfloat16),
            pltpu.VMEM((tiles, 1, capacity), jnp.int32),
            pltpu.VMEM((tiles, features, capacity), jnp.bfloat16),
            pltpu.VMEM((tiles, features, capacity), jnp.bfloat16),
            pltpu.VMEM((features, width), jnp.bfloat16),
            pltpu.VMEM((neigh, width), jnp.int32),
            pltpu.VMEM((neigh, width), jnp.int32),
            pltpu.VMEM((neigh, width), jnp.float32),
            pltpu.VMEM((tiles, width, capacity), jnp.bfloat16),
            pltpu.VMEM((neigh, width, width), jnp.bfloat16),
            pltpu.VMEM((neigh, far, width), jnp.bfloat16),
            pltpu.SemaphoreType.DMA((4,)),
            pltpu.SemaphoreType.DMA((strips,)),
            pltpu.SemaphoreType.DMA((strips,)),
            pltpu.SemaphoreType.DMA((tiles,)),
            pltpu.SemaphoreType.DMA((tiles,)),
            pltpu.SemaphoreType.DMA((tiles,)),
            pltpu.SemaphoreType.DMA((tiles,)),
        ],
        compiler_params=pltpu.CompilerParams(collective_id=0, has_side_effects=True,
                                             vmem_limit_bytes=60 << 20),
        name="phase_rows",
    )(jnp.transpose(stack, (0, 2, 1, 3)), fetch_rows.reshape(tiles, 1, capacity), nbr_tile, nbr_slot, nbr_valid)

    return jnp.transpose(linked, (0, 2, 1, 3))


def solution(mesh):
    in_specs = (
        P(None, ("date", "pol"), None, ("grp", "tile")),
        P(None, ("grp", "tile", "date", "pol")),
        P(None, ("grp", "tile", "date", "pol")),
        P(None, ("grp", "tile", "date", "pol")),
        P(("grp", "tile"), ("date", "pol"), None, None),
    )
    out_specs = P(None, None, None, ("grp", "tile", "date", "pol"))
    return jax.shard_map(functools.partial(body, mesh), mesh=mesh, in_specs=in_specs, out_specs=out_specs,
                         check_vma=False)
```
